32 devices in a mesh: real: 4 (over y, x), cell: 8 (over z, core).
Axes of the slice: x: 2, y: 2, z: 4, core: 2. Of those that a mesh axis runs over, the one named last changes fastest.
Arguments:
- soil_heat_field: float32 [256, 256, 512], P('cell', None, 'real'), may hold values from -250 to 250, as said below
- seed_subspace: float32 [512, 128], replicated, may hold values from -6 to 6
Outputs:
- core_tensor: float32 [256, 256, 128], P('cell', None, 'real')
- mode_factor: float32 [512, 128], replicated
- triangle: float32 [512, 512], replicated
The draws below stay inside these ranges and needn't reach their ends.
Inputs may be any that keep to these rules, and one draw needn't show every extreme that they name: `soil_heat_field`: real values.
All inputs are finite; a program needn't handle non-finite values.
Results may differ from the reference program's by a relative error of at most 0.00024.
Values sent between devices are 32-bit elements; how exact they have to be, the bound alone decides.
A program may use at most 64 MiB of HBM per device.

```python
import math
import jax
import jax.numpy as jnp
from jax import lax

ENSEMBLE_MEMBERS = 512
RANK = 128
SNAPS = 256
ITERS = 3
CELLS = 256


def draw_soil_heat_field(key, part):
    noise_key = jax.random.fold_in(key, 11)
    scale_key = jax.random.fold_in(key, 23)
    field_key = jax.random.fold_in(key, 37)
    loading_key = jax.random.fold_in(key, 41)
    column_scale = jnp.exp(jax.random.uniform(scale_key, (ENSEMBLE_MEMBERS,), jnp.float32, 0.0, math.log(4.0)))
    position = jnp.arange(CELLS, dtype=jnp.float32) / max(CELLS - 1, 1)
    noise_component = jnp.clip(jax.random.normal(noise_key, (CELLS, SNAPS, ENSEMBLE_MEMBERS), jnp.float32), -4.5, 4.5)
    fields = jnp.clip(jax.random.normal(field_key, (4, CELLS, SNAPS), jnp.float32), -3.0, 3.0)
    loadings = jnp.clip(jax.random.normal(loading_key, (4, ENSEMBLE_MEMBERS), jnp.float32), -3.0, 3.0)
    grid_position_series = 1.0 + 2.0 * position
    blended = noise_component + 0.6 * jnp.roll(noise_component, 1, axis=2)
    for factor_index in range(4):
        blended = blended + 0.15 * fields[factor_index][:, :, None] * loadings[factor_index][None, None, :]
    return blended * grid_position_series[:, None, None] * column_scale[None, None, :]


def normal_values(stream_key, dims, deviation, reach, held_as=jnp.bfloat16):
    entries = jax.random.normal(stream_key, dims, jnp.float32) * deviation
    return jnp.minimum(jnp.maximum(entries, -reach), reach).astype(held_as)


def setup_inputs(seed: int = 0) -> dict:
    streams_of = jax.random.split(jax.random.key(seed), 3)
    return {
        "soil_heat_field": draw_soil_heat_field(jax.random.fold_in(streams_of[2], 71), 0),
        "seed_subspace": normal_values(streams_of[1], (ENSEMBLE_MEMBERS, RANK), 1.0, 6.0, jnp.float32),
    }


def gram_of(array_operand):
    return lax.dot_general(array_operand.astype(jnp.float32), array_operand.astype(jnp.float32), (((0,), (0,)), ((), ())), precision=lax.Precision.HIGHEST, preferred_element_type=jnp.float32)

def orthonormal(gram, seed_subspace):
    basis_block = seed_subspace
    for step_index in range(ITERS):
        imaged = jnp.dot(gram.astype(jnp.float32), basis_block.astype(jnp.float32), precision=lax.Precision.HIGHEST, preferred_element_type=jnp.float32)
        cholesky_lower = jnp.linalg.cholesky(gram_of(imaged))
        basis_block = lax.linalg.triangular_solve(cholesky_lower, imaged, left_side=False, lower=True, transpose_a=True)
    return basis_block

def reference(soil_heat_field, seed_subspace):
    flattened_mode_array = soil_heat_field.reshape(-1, ENSEMBLE_MEMBERS)
    gram = gram_of(flattened_mode_array) / (CELLS * SNAPS)
    triangle = jnp.linalg.cholesky(gram).T
    mode_factor = orthonormal(gram, seed_subspace)
    core_tensor = jnp.dot(flattened_mode_array.astype(jnp.float32), mode_factor.astype(jnp.float32), precision=lax.Precision.HIGHEST, preferred_element_type=jnp.float32)
    return (core_tensor.reshape(CELLS, SNAPS, RANK), mode_factor, triangle)
```

```python
import functools
import jax
import jax.numpy as jnp
from jax import lax
from jax.experimental import pallas as pl
from jax.experimental.pallas import tpu as pltpu
from jax.sharding import PartitionSpec as P

ITERS = 3
PANEL = 32
GROUP = 8
HI = lax.Precision.HIGHEST


def mm(a, b, dims=((1,), (0,))):
    return lax.dot_general(
        a, b, (dims, ((), ())), precision=HI, preferred_element_type=jnp.float32
    )


def eliminate(panel, first_lane):
    size = panel.shape[0]
    done, pivots = [], []
    rest = panel
    for g in range(0, size, GROUP):
        rows = [rest[i : i + 1, :] for i in range(GROUP)]
        lane = first_lane + g
        cell = {
            (i, k): rows[i][:, lane + k : lane + k + 1]
            for i in range(GROUP)
            for k in range(i, GROUP)
        }
        below = rest[GROUP:, :]
        more = below.shape[0] > 0
        if more:
            cols = [below[:, lane + k : lane + k + 1] for k in range(GROUP)]
        for i in range(GROUP):
            inverse = 1.0 / cell[i, i]
            pivots.append(cell[i, i])
            for k in range(i + 1, GROUP):
                factor = cell[i, k] * inverse
                for q in range(k, GROUP):
                    cell[k, q] = cell[k, q] - factor * cell[i, q]
                rows[k] = rows[k] - factor * rows[i]
                if more:
                    cols[k] = cols[k] - cols[i] * factor
            if more:
                below = below - cols[i] * (rows[i] * inverse)
        done += rows
        rest = below
    return [u * lax.rsqrt(p) for u, p in zip(done, pivots)]


def factor_panels(works, outs, size):
    for p in range(0, size, PANEL):
        for work, out in zip(works, outs):
            rows = jnp.concatenate(eliminate(work[p : p + PANEL, :], p), axis=0)
            out[p : p + PANEL, :] = rows
            if p + PANEL < size:
                left = size - p - PANEL
                drop = mm(rows[:, :size], rows, ((0,), (0,)))
                work[p + PANEL :, :] = work[p + PANEL :, :] - drop[p + PANEL :, :]


def factors_kernel(gram_ref, seed_ref, basis_ref, tri_ref, rest, image, work_a, out_a, work_b, out_b):
    size = seed_ref.shape[1]
    total = gram_ref.shape[0]
    row = lax.broadcasted_iota(jnp.int32, (size, size), 0)
    col = lax.broadcasted_iota(jnp.int32, (size, size), 1)
    eye = jnp.where(row == col, 1.0, 0.0).astype(jnp.float32)
    rest[...] = gram_ref[...]
    basis_ref[...] = seed_ref[...]

    def triangle_start(block):
        at = pl.multiple_of(block * size, size)
        work_b[:, :size] = rest[pl.ds(at, size), pl.ds(at, size)]
        work_b[:, size:] = eye

    def triangle_end(block):
        at = pl.multiple_of(block * size, size)
        inverse = jnp.where(row >= col, out_b[:, size:], 0.0)
        strip = mm(inverse, rest[pl.ds(at, size), :])
        rows = at + lax.broadcasted_iota(jnp.int32, (size, total), 0)
        cols = lax.broadcasted_iota(jnp.int32, (size, total), 1)
        strip = jnp.where(cols >= rows, strip, 0.0)
        tri_ref[pl.ds(at, size), :] = strip
        return strip

    def step(index, carry):
        image[...] = mm(gram_ref[...], basis_ref[...])
        work_a[:, :size] = mm(image[...], image[...], ((0,), (0,)))
        work_a[:, size:] = eye
        triangle_start(index)
        factor_panels([work_a, work_b], [out_a, out_b], size)
        inverse = jnp.where(row >= col, out_a[:, size:], 0.0)
        basis_ref[...] = mm(image[...], inverse, ((1,), (1,)))
        strip = triangle_end(index)
        rest[...] = rest[...] - mm(strip, strip, ((0,), (0,)))
        return carry

    blocks = total // size
    lax.fori_loop(0, ITERS, step, 0)
    for block in range(ITERS, blocks):
        triangle_start(block)
        factor_panels([work_b], [out_b], size)
        strip = triangle_end(block)
        if block + 1 < blocks:
            rest[...] = rest[...] - mm(strip, strip, ((0,), (0,)))


def factors(gram, seed_subspace):
    total, size = seed_subspace.shape
    vmem = pl.BlockSpec(memory_space=pltpu.VMEM)
    return pl.pallas_call(
        factors_kernel,
        out_shape=(
            jax.ShapeDtypeStruct((total, size), jnp.float32),
            jax.ShapeDtypeStruct((total, total), jnp.float32),
        ),
        in_specs=[vmem] * 2,
        out_specs=[vmem] * 2,
        scratch_shapes=[
            pltpu.VMEM((total, total), jnp.float32),
            pltpu.VMEM((total, size), jnp.float32),
        ]
        + [pltpu.VMEM((size, 2 * size), jnp.float32)] * 4,
        compiler_params=pltpu.CompilerParams(vmem_limit_bytes=32 * 1024 * 1024),
    )(gram, seed_subspace)


def local(soil_heat_field, seed_subspace):
    permuted_array = lax.all_to_all(
        soil_heat_field, "real", split_axis=1, concat_axis=2, tiled=True
    )
    flat = permuted_array.reshape(-1, permuted_array.shape[2])
    total_rows = flat.shape[0] * lax.axis_size(("real", "cell"))
    summed = lax.psum(mm(flat, flat, ((0,), (0,))) / total_rows, ("real", "cell"))
    mode_factor, triangle = factors(summed, seed_subspace)
    compressed = mm(flat, mode_factor).reshape(
        permuted_array.shape[0], permuted_array.shape[1], -1
    )
    core_tensor = lax.all_to_all(compressed, "real", split_axis=2, concat_axis=1, tiled=True)
    return (core_tensor, mode_factor, triangle)


def solution(mesh):
    return jax.shard_map(
        local,
        mesh=mesh,
        in_specs=(P("cell", None, "real"), P()),
        out_specs=(P("cell", None, "real"), P(), P()),
        check_vma=False,
    )
```

```python
import functools
import jax
import jax.numpy as jnp
from jax import lax
from jax.experimental import pallas as pl
from jax.experimental.pallas import tpu as pltpu
from jax.sharding import PartitionSpec as P

ITERS = 3
PANEL = 32
GROUP = 8
HI = lax.Precision.HIGHEST


def mm(a, b, dims=((1,), (0,))):
    return lax.dot_general(
        a, b, (dims, ((), ())), precision=HI, preferred_element_type=jnp.float32
    )


def upper_blocks(count):
    return [(i, j) for i in range(count) for j in range(i, count)]


def spread(tile, lane):
    return jnp.broadcast_to(tile[:, lane : lane + 1], tile.shape)


def eliminate(tiles, first_lane):
    sub = lax.broadcasted_iota(jnp.int32, tiles[0][0].shape, 0)
    done = []
    for g in range(len(tiles)):
        lane = first_lane + g * GROUP
        head, rest = tiles[g], tiles[g + 1 :]
        rows = [
            [jnp.broadcast_to(half[i : i + 1, :], half.shape) for half in head]
            for i in range(GROUP)
        ]
        cell = {
            (i, k): spread(rows[i][0], lane + k)
            for i in range(GROUP)
            for k in range(i, GROUP)
        }
        cols = [[spread(t[0], lane + k) for t in rest] for k in range(GROUP)]
        for i in range(GROUP):
            inverse = 1.0 / cell[i, i]
            for k in range(i + 1, GROUP):
                factor = cell[i, k] * inverse
                for q in range(k, GROUP):
                    cell[k, q] = cell[k, q] - factor * cell[i, q]
                rows[k] = [x - factor * y for x, y in zip(rows[k], rows[i])]
                cols[k] = [x - factor * y for x, y in zip(cols[k], cols[i])]
            scaled = [y * inverse for y in rows[i]]
            rest = [
                tuple(x - c * y for x, y in zip(t, scaled)) for t, c in zip(rest, cols[i])
            ]
        tiles = tiles[: g + 1] + rest
        halves = []
        for h in range(2):
            value = rows[0][h] * lax.rsqrt(cell[0, 0])
            for i in range(1, GROUP):
                value = jnp.where(sub == i, rows[i][h] * lax.rsqrt(cell[i, i]), value)
            halves.append(value)
        done.append(halves)
    return done


def factor_panels(works, outs, size):
    for p in range(0, size, PANEL):
        for work, out in zip(works, outs):
            tiles = [
                (work[q : q + GROUP, :size], work[q : q + GROUP, size:])
                for q in range(p, p + PANEL, GROUP)
            ]
            for g, (left, right) in enumerate(eliminate(tiles, p)):
                at = p + g * GROUP
                out[at : at + GROUP, :size] = left
                out[at : at + GROUP, size:] = right
            if p + PANEL < size:
                rows = out[p : p + PANEL, :]
                drop = mm(rows[:, :size], rows, ((0,), (0,)))
                work[p + PANEL :, :] = work[p + PANEL :, :] - drop[p + PANEL :, :]


def factors_kernel(packed_ref, seed_ref, basis_ref, tri_ref, gram_ref, rest, image, work_a, out_a, work_b, out_b):
    size = seed_ref.shape[1]
    total = seed_ref.shape[0]
    for number, (i, j) in enumerate(upper_blocks(total // size)):
        block = packed_ref[number * size : (number + 1) * size, :]
        gram_ref[i * size : (i + 1) * size, j * size : (j + 1) * size] = block
        if i != j:
            gram_ref[j * size : (j + 1) * size, i * size : (i + 1) * size] = block.T
    row = lax.broadcasted_iota(jnp.int32, (size, size), 0)
    col = lax.broadcasted_iota(jnp.int32, (size, size), 1)
    eye = jnp.where(row == col, 1.0, 0.0).astype(jnp.float32)
    rest[...] = gram_ref[...]
    basis_ref[...] = seed_ref[...]

    def triangle_start(block):
        at = pl.multiple_of(block * size, size)
        work_b[:, :size] = rest[pl.ds(at, size), pl.ds(at, size)]
        work_b[:, size:] = eye

    def triangle_end(block):
        at = pl.multiple_of(block * size, size)
        inverse = jnp.where(row >= col, out_b[:, size:], 0.0)
        strip = mm(inverse, rest[pl.ds(at, size), :])
        rows = at + lax.broadcasted_iota(jnp.int32, (size, total), 0)
        cols = lax.broadcasted_iota(jnp.int32, (size, total), 1)
        strip = jnp.where(cols >= rows, strip, 0.0)
        tri_ref[pl.ds(at, size), :] = strip
        return strip

    def step(index, carry):
        image[...] = mm(gram_ref[...], basis_ref[...])
        work_a[:, :size] = mm(image[...], image[...], ((0,), (0,)))
        work_a[:, size:] = eye
        triangle_start(index)
        factor_panels([work_a, work_b], [out_a, out_b], size)
        inverse = jnp.where(row >= col, out_a[:, size:], 0.0)
        basis_ref[...] = mm(image[...], inverse, ((1,), (1,)))
        strip = triangle_end(index)
        rest[...] = rest[...] - mm(strip, strip, ((0,), (0,)))
        return carry

    blocks = total // size
    lax.fori_loop(0, ITERS, step, 0)
    for block in range(ITERS, blocks):
        triangle_start(block)
        factor_panels([work_b], [out_b], size)
        strip = triangle_end(block)
        if block + 1 < blocks:
            rest[...] = rest[...] - mm(strip, strip, ((0,), (0,)))


def factors(packed, seed_subspace):
    total, size = seed_subspace.shape
    vmem = pl.BlockSpec(memory_space=pltpu.VMEM)
    return pl.pallas_call(
        factors_kernel,
        out_shape=(
            jax.ShapeDtypeStruct((total, size), jnp.float32),
            jax.ShapeDtypeStruct((total, total), jnp.float32),
        ),
        in_specs=[vmem] * 2,
        out_specs=[vmem] * 2,
        scratch_shapes=[
            pltpu.VMEM((total, total), jnp.float32),
            pltpu.VMEM((total, total), jnp.float32),
            pltpu.VMEM((total, size), jnp.float32),
        ]
        + [pltpu.VMEM((size, 2 * size), jnp.float32)] * 4,
        compiler_params=pltpu.CompilerParams(vmem_limit_bytes=32 * 1024 * 1024),
    )(packed, seed_subspace)


MESH = pl.DeviceIdType.MESH


def greet(peers):
    barrier = pltpu.get_barrier_semaphore()
    for peer in peers:
        pl.semaphore_signal(barrier, inc=1, device_id=peer, device_id_type=MESH)
    pl.semaphore_wait(barrier, len(peers))


def send(src, dst, sems, slot, peer):
    copy = pltpu.make_async_remote_copy(
        src_ref=src,
        dst_ref=dst,
        send_sem=sems[0].at[slot],
        recv_sem=sems[1].at[slot],
        device_id=peer,
        device_id_type=MESH,
    )
    copy.start()
    return copy


def gram_kernel(
    reals, depth, chunks, field_ref, held_ref, out_ref, acc, packed,
    from_core, half, from_real, quarter, from_depth, own_sem,
    field_send, field_recv, sum_send, sum_recv, gather_send, gather_recv,
):
    r, cell = lax.axis_index("real"), lax.axis_index("cell")
    z, c = cell // 2, cell % 2
    cells, snaps, width = held_ref.shape[1:]
    real_peers = [lax.rem(r + d, reals) for d in range(1, reals)]
    depth_peers = [lax.rem(z + d, depth) for d in range(1, depth)]
    to_core = {"real": r, "cell": z * 2 + 1 - c}
    to_real = [{"real": q, "cell": cell} for q in real_peers]
    to_depth = [{"real": r, "cell": q * 2 + c} for q in depth_peers]
    greet([to_core] + to_real + to_depth)

    step = cells // chunks
    moves = []
    for k in range(chunks):
        own = pltpu.make_async_copy(
            field_ref.at[pl.ds(k * step, step), pl.ds(r * snaps, snaps), :],
            held_ref.at[r, pl.ds(k * step, step)],
            own_sem.at[k],
        )
        own.start()
        moves.append([own])
        for d, (q, peer) in enumerate(zip(real_peers, to_real)):
            moves[k].append(
                send(
                    field_ref.at[pl.ds(k * step, step), pl.ds(q * snaps, snaps), :],
                    held_ref.at[r, pl.ds(k * step, step)],
                    (field_send, field_recv),
                    k * (reals - 1) + d,
                    peer,
                )
            )
    total_rows = cells * snaps * reals * depth * 2
    for k in range(chunks):
        moves[k][0].wait()
        for copy in moves[k][1:]:
            copy.wait_recv()
        rows = jnp.concatenate(
            [
                held_ref[s, k * step : (k + 1) * step].reshape(step * snaps, width)
                for s in range(reals)
            ],
            axis=1,
        )
        part = mm(rows, rows, ((0,), (0,)))
        acc[...] = part if k == 0 else acc[...] + part
    for k in range(chunks):
        for copy in moves[k][1:]:
            copy.wait_send()

    blocks = upper_blocks(reals)
    for number, (i, j) in enumerate(blocks):
        packed[number * width : (number + 1) * width, :] = (
            acc[i * width : (i + 1) * width, j * width : (j + 1) * width] / total_rows
        )
    used = len(blocks) * width
    if packed.shape[0] > used:
        packed[used:, :] = jnp.zeros((packed.shape[0] - used, width), jnp.float32)

    sums = (sum_send, sum_recv)
    h, q, e = half.shape[0], quarter.shape[0], from_depth.shape[1]
    copy = send(packed.at[pl.ds((1 - c) * h, h)], from_core, sums, 0, to_core)
    copy.wait()
    half[...] = packed[pl.ds(pl.multiple_of(c * h, 8), h), :] + from_core[...]
    copies = [
        send(half.at[pl.ds(p * q, q)], from_real.at[d], sums, 1 + d, peer)
        for d, (p, peer) in enumerate(zip(real_peers, to_real))
    ]
    for copy in copies:
        copy.wait()
    value = half[pl.ds(pl.multiple_of(r * q, 8), q), :]
    for d in range(reals - 1):
        value = value + from_real[d]
    quarter[...] = value
    copies = [
        send(quarter.at[pl.ds(p * e, e)], from_depth.at[d], sums, reals + d, peer)
        for d, (p, peer) in enumerate(zip(depth_peers, to_depth))
    ]
    for copy in copies:
        copy.wait()
    value = quarter[pl.ds(pl.multiple_of(z * e, 8), e), :]
    for d in range(depth - 1):
        value = value + from_depth[d]

    gathers = (gather_send, gather_recv)
    base = c * h + r * q
    mine = pl.multiple_of(base + z * e, 8)
    out_ref[pl.ds(mine, e), :] = value
    for first, count, slot, peers in (
        (mine, e, reals, to_depth),
        (base, q, 1, to_real),
        (c * h, h, 0, [to_core]),
    ):
        part = out_ref.at[pl.ds(first, count)]
        copies = [send(part, part, gathers, slot + d, peer) for d, peer in enumerate(peers)]
        for copy in copies:
            copy.wait()


def gathered_gram(field, reals, depth):
    cells, snaps, width = field.shape
    snaps //= reals
    chunks = 4
    used = len(upper_blocks(reals)) * width
    e = -(-used // (2 * reals * depth * 8)) * 8
    q = e * depth
    h = q * reals
    peers = reals + depth - 1
    f32 = jnp.float32
    dma = pltpu.SemaphoreType.DMA
    vmem = pl.BlockSpec(memory_space=pltpu.VMEM)
    return pl.pallas_call(
        functools.partial(gram_kernel, reals, depth, chunks),
        out_shape=(
            jax.ShapeDtypeStruct((reals, cells, snaps, width), f32),
            jax.ShapeDtypeStruct((2 * h, width), f32),
        ),
        in_specs=[pl.BlockSpec(memory_space=pl.ANY)],
        out_specs=[vmem] * 2,
        scratch_shapes=[
            pltpu.VMEM((reals * width, reals * width), f32),
            pltpu.VMEM((2 * h, width), f32),
            pltpu.VMEM((h, width), f32),
            pltpu.VMEM((h, width), f32),
            pltpu.VMEM((reals - 1, q, width), f32),
            pltpu.VMEM((q, width), f32),
            pltpu.VMEM((depth - 1, e, width), f32),
            dma((chunks,)),
            dma((chunks * (reals - 1),)),
            dma((chunks * (reals - 1),)),
            dma((peers,)),
            dma((peers,)),
            dma((peers,)),
            dma((peers,)),
        ],
        compiler_params=pltpu.CompilerParams(
            collective_id=0, has_side_effects=True, vmem_limit_bytes=40 * 1024 * 1024
        ),
    )(field)


def core_kernel(reals, held_ref, basis_ref, got_ref, sending, send_sem, recv_sem):
    r, cell = lax.axis_index("real"), lax.axis_index("cell")
    peers = [lax.rem(r + d, reals) for d in range(1, reals)]
    places = [{"real": q, "cell": cell} for q in peers]
    greet(places)
    rows, width = held_ref.shape[1:]
    ranks = got_ref.shape[1]
    parts = 4
    count = rows // parts
    copies = []
    for part in range(parts):
        first = part * count
        value = mm(held_ref[0, first : first + count, :], basis_ref[:width, :])
        for s in range(1, reals):
            value = value + mm(
                held_ref[s, first : first + count, :], basis_ref[s * width : (s + 1) * width, :]
            )
        turned = value.T
        for s in range(reals):
            sending[s, :, first : first + count] = turned[s * ranks : (s + 1) * ranks, :]
        lanes = pl.ds(first, count)
        for d, (q, place) in enumerate(zip(peers, places)):
            copies.append(
                send(
                    sending.at[q, :, lanes],
                    got_ref.at[r, :, lanes],
                    (send_sem, recv_sem),
                    part * (reals - 1) + d,
                    place,
                )
            )
    got_ref[pl.ds(r, 1)] = sending[pl.ds(r, 1)]
    for copy in copies:
        copy.wait()


def projected(held, basis, reals):
    rows, width = held.shape[1:]
    rank = basis.shape[1]
    shape = (reals, rank // reals, rows)
    vmem = pl.BlockSpec(memory_space=pltpu.VMEM)
    return pl.pallas_call(
        functools.partial(core_kernel, reals),
        out_shape=jax.ShapeDtypeStruct(shape, jnp.float32),
        in_specs=[vmem] * 2,
        out_specs=vmem,
        scratch_shapes=[
            pltpu.VMEM(shape, jnp.float32),
            pltpu.SemaphoreType.DMA((4 * (reals - 1),)),
            pltpu.SemaphoreType.DMA((4 * (reals - 1),)),
        ],
        compiler_params=pltpu.CompilerParams(
            collective_id=1, has_side_effects=True, vmem_limit_bytes=40 * 1024 * 1024
        ),
    )(held, basis)


def local(soil_heat_field, seed_subspace):
    reals, depth = lax.axis_size("real"), lax.axis_size("cell") // 2
    held, packed = gathered_gram(soil_heat_field, reals, depth)
    mode_factor, triangle = factors(packed, seed_subspace)
    cells, snaps, width = held.shape[1:]
    got = projected(held.reshape(reals, cells * snaps, width), mode_factor, reals)
    core_tensor = got.reshape(reals, -1, cells, snaps).transpose(2, 0, 3, 1)
    return (core_tensor.reshape(cells, reals * snaps, -1), mode_factor, triangle)


def solution(mesh):
    return jax.shard_map(
        local,
        mesh=mesh,
        in_specs=(P("cell", None, "real"), P()),
        out_specs=(P("cell", None, "real"), P(), P()),
        check_vma=False,
    )
```

```python
import functools
import jax
import jax.numpy as jnp
from jax import lax
from jax.experimental import pallas as pl
from jax.experimental.pallas import tpu as pltpu
from jax.sharding import PartitionSpec as P

ITERS = 3
PANEL = 32
GROUP = 8
HI = lax.Precision.HIGHEST


def mm(a, b, dims=((1,), (0,))):
    return lax.dot_general(
        a, b, (dims, ((), ())), precision=HI, preferred_element_type=jnp.float32
    )


def upper_blocks(count):
    return [(i, j) for i in range(count) for j in range(i, count)]


def spread(tile, lane):
    return jnp.broadcast_to(tile[:, lane : lane + 1], tile.shape)


def reciprocal(x):
    guess = pl.reciprocal(x, approx=True)
    return guess * (2.0 - x * guess)


def eliminate(tiles, first_lane):
    sub = lax.broadcasted_iota(jnp.int32, tiles[0][0].shape, 0)
    done = []
    for g in range(len(tiles)):
        lane = first_lane + g * GROUP
        head, rest = tiles[g], tiles[g + 1 :]
        rows = [
            [jnp.broadcast_to(half[i : i + 1, :], half.shape) for half in head]
            for i in range(GROUP)
        ]
        cell = {
            (i, k): spread(rows[i][0], lane + k)
            for i in range(GROUP)
            for k in range(i, GROUP)
        }
        cols = [[spread(t[0], lane + k) for t in rest] for k in range(GROUP)]
        for i in range(GROUP):
            inverse = reciprocal(cell[i, i])
            for k in range(i + 1, GROUP):
                factor = cell[i, k] * inverse
                for q in range(k, GROUP):
                    cell[k, q] = cell[k, q] - factor * cell[i, q]
                rows[k] = [x - factor * y for x, y in zip(rows[k], rows[i])]
                cols[k] = [x - factor * y for x, y in zip(cols[k], cols[i])]
            scaled = [y * inverse for y in rows[i]]
            rest = [
                tuple(x - c * y for x, y in zip(t, scaled)) for t, c in zip(rest, cols[i])
            ]
        tiles = tiles[: g + 1] + rest
        pivots, halves = cell[0, 0], rows[0]
        for i in range(1, GROUP):
            here = sub == i
            pivots = jnp.where(here, cell[i, i], pivots)
            halves = [jnp.where(here, x, y) for x, y in zip(rows[i], halves)]
        scale = lax.rsqrt(pivots)
        halves = [x * scale for x in halves]
        done.append(halves)
    return done


def factor_panels(works, outs, size):
    for p in range(0, size, PANEL):
        for work, out in zip(works, outs):
            tiles = [
                (work[q : q + GROUP, :size], work[q : q + GROUP, size:])
                for q in range(p, p + PANEL, GROUP)
            ]
            for g, (left, right) in enumerate(eliminate(tiles, p)):
                at = p + g * GROUP
                out[at : at + GROUP, :size] = left
                out[at : at + GROUP, size:] = right
            if p + PANEL < size:
                rows = out[p : p + PANEL, :]
                drop = mm(rows[:, :size], rows, ((0,), (0,)))
                work[p + PANEL :, :] = work[p + PANEL :, :] - drop[p + PANEL :, :]


def factors_kernel(packed_ref, seed_ref, basis_ref, tri_ref, last_ref, gram_ref, rest, image, work_a, out_a, work_b, out_b):
    size = seed_ref.shape[1]
    total = seed_ref.shape[0]
    for number, (i, j) in enumerate(upper_blocks(total // size)):
        block = packed_ref[number * size : (number + 1) * size, :]
        gram_ref[i * size : (i + 1) * size, j * size : (j + 1) * size] = block
        if i != j:
            gram_ref[j * size : (j + 1) * size, i * size : (i + 1) * size] = block.T
    row = lax.broadcasted_iota(jnp.int32, (size, size), 0)
    col = lax.broadcasted_iota(jnp.int32, (size, size), 1)
    eye = jnp.where(row == col, 1.0, 0.0).astype(jnp.float32)
    rest[...] = gram_ref[...]
    basis_ref[...] = seed_ref[...]

    def triangle_start(block):
        at = pl.multiple_of(block * size, size)
        work_b[:, :size] = rest[pl.ds(at, size), pl.ds(at, size)]
        work_b[:, size:] = eye

    def triangle_end(block):
        at = pl.multiple_of(block * size, size)
        inverse = jnp.where(row >= col, out_b[:, size:], 0.0)
        strip = mm(inverse, rest[pl.ds(at, size), :])
        rows = at + lax.broadcasted_iota(jnp.int32, (size, total), 0)
        cols = lax.broadcasted_iota(jnp.int32, (size, total), 1)
        strip = jnp.where(cols >= rows, strip, 0.0)
        tri_ref[pl.ds(at, size), :] = strip
        return strip

    def step(index, carry):
        image[...] = mm(gram_ref[...], basis_ref[...])
        work_a[:, :size] = mm(image[...], image[...], ((0,), (0,)))
        work_a[:, size:] = eye
        triangle_start(index)
        factor_panels([work_a, work_b], [out_a, out_b], size)
        inverse = jnp.where(row >= col, out_a[:, size:], 0.0)
        basis_ref[...] = mm(image[...], inverse, ((1,), (1,)))
        strip = triangle_end(index)
        rest[...] = rest[...] - mm(strip, strip, ((0,), (0,)))
        return carry

    blocks = total // size
    lax.fori_loop(0, ITERS, step, 0)
    for block in range(ITERS, blocks - 1):
        triangle_start(block)
        factor_panels([work_b], [out_b], size)
        strip = triangle_end(block)
        rest[...] = rest[...] - mm(strip, strip, ((0,), (0,)))
    tri_ref[total - size :, :] = jnp.zeros((size, total), jnp.float32)
    last_ref[...] = rest[total - size :, total - size :]


def factors(packed, seed_subspace):
    total, size = seed_subspace.shape
    vmem = pl.BlockSpec(memory_space=pltpu.VMEM)
    return pl.pallas_call(
        factors_kernel,
        out_shape=(
            jax.ShapeDtypeStruct((total, size), jnp.float32),
            jax.ShapeDtypeStruct((total, total), jnp.float32),
            jax.ShapeDtypeStruct((size, size), jnp.float32),
        ),
        in_specs=[vmem] * 2,
        out_specs=[vmem] * 3,
        scratch_shapes=[
            pltpu.VMEM((total, total), jnp.float32),
            pltpu.VMEM((total, total), jnp.float32),
            pltpu.VMEM((total, size), jnp.float32),
        ]
        + [pltpu.VMEM((size, 2 * size), jnp.float32)] * 4,
        compiler_params=pltpu.CompilerParams(vmem_limit_bytes=32 * 1024 * 1024),
    )(packed, seed_subspace)


MESH = pl.DeviceIdType.MESH


def greet(peers):
    barrier = pltpu.get_barrier_semaphore()
    for peer in peers:
        pl.semaphore_signal(barrier, inc=1, device_id=peer, device_id_type=MESH)
    pl.semaphore_wait(barrier, len(peers))


def send(src, dst, sems, slot, peer):
    copy = pltpu.make_async_remote_copy(
        src_ref=src,
        dst_ref=dst,
        send_sem=sems[0].at[slot],
        recv_sem=sems[1].at[slot],
        device_id=peer,
        device_id_type=MESH,
    )
    copy.start()
    return copy


def gram_kernel(
    reals, depth, chunks, field_ref, held_ref, out_ref, acc, packed,
    from_core, half, from_real, quarter, from_depth, own_sem,
    field_send, field_recv, sum_send, sum_recv, gather_send, gather_recv,
):
    r, cell = lax.axis_index("real"), lax.axis_index("cell")
    z, c = cell // 2, cell % 2
    cells, snaps, width = held_ref.shape[1:]
    real_peers = [lax.rem(r + d, reals) for d in range(1, reals)]
    depth_peers = [lax.rem(z + d, depth) for d in range(1, depth)]
    to_core = {"real": r, "cell": z * 2 + 1 - c}
    to_real = [{"real": q, "cell": cell} for q in real_peers]
    to_depth = [{"real": r, "cell": q * 2 + c} for q in depth_peers]
    greet([to_core] + to_real + to_depth)

    step = cells // chunks
    moves = []
    for k in range(chunks):
        own = pltpu.make_async_copy(
            field_ref.at[pl.ds(k * step, step), pl.ds(r * snaps, snaps), :],
            held_ref.at[r, pl.ds(k * step, step)],
            own_sem.at[k],
        )
        own.start()
        moves.append([own])
        for d, (q, peer) in enumerate(zip(real_peers, to_real)):
            moves[k].append(
                send(
                    field_ref.at[pl.ds(k * step, step), pl.ds(q * snaps, snaps), :],
                    held_ref.at[r, pl.ds(k * step, step)],
                    (field_send, field_recv),
                    k * (reals - 1) + d,
                    peer,
                )
            )
    total_rows = cells * snaps * reals * depth * 2
    for k in range(chunks):
        moves[k][0].wait()
        for copy in moves[k][1:]:
            copy.wait_recv()
        rows = jnp.concatenate(
            [
                held_ref[s, k * step : (k + 1) * step].reshape(step * snaps, width)
                for s in range(reals)
            ],
            axis=1,
        )
        part = mm(rows, rows, ((0,), (0,)))
        acc[...] = part if k == 0 else acc[...] + part
    for k in range(chunks):
        for copy in moves[k][1:]:
            copy.wait_send()

    blocks = upper_blocks(reals)
    for number, (i, j) in enumerate(blocks):
        packed[number * width : (number + 1) * width, :] = (
            acc[i * width : (i + 1) * width, j * width : (j + 1) * width] / total_rows
        )
    used = len(blocks) * width
    if packed.shape[0] > used:
        packed[used:, :] = jnp.zeros((packed.shape[0] - used, width), jnp.float32)

    sums = (sum_send, sum_recv)
    h, q, e = half.shape[0], quarter.shape[0], from_depth.shape[1]
    copy = send(packed.at[pl.ds((1 - c) * h, h)], from_core, sums, 0, to_core)
    copy.wait()
    half[...] = packed[pl.ds(pl.multiple_of(c * h, 8), h), :] + from_core[...]
    copies = [
        send(half.at[pl.ds(p * q, q)], from_real.at[d], sums, 1 + d, peer)
        for d, (p, peer) in enumerate(zip(real_peers, to_real))
    ]
    for copy in copies:
        copy.wait()
    value = half[pl.ds(pl.multiple_of(r * q, 8), q), :]
    for d in range(reals - 1):
        value = value + from_real[d]
    quarter[...] = value
    copies = [
        send(quarter.at[pl.ds(p * e, e)], from_depth.at[d], sums, reals + d, peer)
        for d, (p, peer) in enumerate(zip(depth_peers, to_depth))
    ]
    for copy in copies:
        copy.wait()
    value = quarter[pl.ds(pl.multiple_of(z * e, 8), e), :]
    for d in range(depth - 1):
        value = value + from_depth[d]

    gathers = (gather_send, gather_recv)
    base = c * h + r * q
    mine = pl.multiple_of(base + z * e, 8)
    out_ref[pl.ds(mine, e), :] = value
    for first, count, slot, peers in (
        (mine, e, reals, to_depth),
        (base, q, 1, to_real),
        (c * h, h, 0, [to_core]),
    ):
        part = out_ref.at[pl.ds(first, count)]
        copies = [send(part, part, gathers, slot + d, peer) for d, peer in enumerate(peers)]
        for copy in copies:
            copy.wait()


def gathered_gram(field, reals, depth):
    cells, snaps, width = field.shape
    snaps //= reals
    chunks = 8
    used = len(upper_blocks(reals)) * width
    e = -(-used // (2 * reals * depth * 8)) * 8
    q = e * depth
    h = q * reals
    peers = reals + depth - 1
    f32 = jnp.float32
    dma = pltpu.SemaphoreType.DMA
    vmem = pl.BlockSpec(memory_space=pltpu.VMEM)
    return pl.pallas_call(
        functools.partial(gram_kernel, reals, depth, chunks),
        out_shape=(
            jax.ShapeDtypeStruct((reals, cells, snaps, width), f32),
            jax.ShapeDtypeStruct((2 * h, width), f32),
        ),
        in_specs=[pl.BlockSpec(memory_space=pl.ANY)],
        out_specs=[vmem] * 2,
        scratch_shapes=[
            pltpu.VMEM((reals * width, reals * width), f32),
            pltpu.VMEM((2 * h, width), f32),
            pltpu.VMEM((h, width), f32),
            pltpu.VMEM((h, width), f32),
            pltpu.VMEM((reals - 1, q, width), f32),
            pltpu.VMEM((q, width), f32),
            pltpu.VMEM((depth - 1, e, width), f32),
            dma((chunks,)),
            dma((chunks * (reals - 1),)),
            dma((chunks * (reals - 1),)),
            dma((peers,)),
            dma((peers,)),
            dma((peers,)),
            dma((peers,)),
        ],
        compiler_params=pltpu.CompilerParams(
            collective_id=0, has_side_effects=True, vmem_limit_bytes=60 * 1024 * 1024
        ),
    )(field)


def core_kernel(
    reals, held_ref, basis_ref, last_ref, got_ref, corner_ref,
    sending, work, out, send_sem, recv_sem,
):
    r, cell = lax.axis_index("real"), lax.axis_index("cell")
    peers = [lax.rem(r + d, reals) for d in range(1, reals)]
    places = [{"real": q, "cell": cell} for q in peers]
    greet(places)
    rows, width = held_ref.shape[1:]
    ranks = got_ref.shape[1]
    parts = 4
    count = rows // parts
    copies = []
    for part in range(parts):
        first = part * count
        value = mm(held_ref[0, first : first + count, :], basis_ref[:width, :])
        for s in range(1, reals):
            value = value + mm(
                held_ref[s, first : first + count, :], basis_ref[s * width : (s + 1) * width, :]
            )
        turned = value.T
        for s in range(reals):
            sending[s, :, first : first + count] = turned[s * ranks : (s + 1) * ranks, :]
        lanes = pl.ds(first, count)
        for d, (q, place) in enumerate(zip(peers, places)):
            copies.append(
                send(
                    sending.at[q, :, lanes],
                    got_ref.at[r, :, lanes],
                    (send_sem, recv_sem),
                    part * (reals - 1) + d,
                    place,
                )
            )
    got_ref[pl.ds(r, 1)] = sending[pl.ds(r, 1)]
    size = last_ref.shape[0]
    row = lax.broadcasted_iota(jnp.int32, (size, size), 0)
    col = lax.broadcasted_iota(jnp.int32, (size, size), 1)
    work[:, :size] = last_ref[...]
    work[:, size:] = jnp.where(row == col, 1.0, 0.0).astype(jnp.float32)
    factor_panels([work], [out], size)
    corner_ref[...] = jnp.where(col >= row, out[:, :size], 0.0)
    for copy in copies:
        copy.wait()


def projected(held, basis, last, reals):
    rows, width = held.shape[1:]
    rank = basis.shape[1]
    size = last.shape[0]
    shape = (reals, rank // reals, rows)
    vmem = pl.BlockSpec(memory_space=pltpu.VMEM)
    return pl.pallas_call(
        functools.partial(core_kernel, reals),
        out_shape=(
            jax.ShapeDtypeStruct(shape, jnp.float32),
            jax.ShapeDtypeStruct(last.shape, jnp.float32),
        ),
        in_specs=[vmem] * 3,
        out_specs=[vmem] * 2,
        scratch_shapes=[
            pltpu.VMEM(shape, jnp.float32),
            pltpu.VMEM((size, 2 * size), jnp.float32),
            pltpu.VMEM((size, 2 * size), jnp.float32),
            pltpu.SemaphoreType.DMA((4 * (reals - 1),)),
            pltpu.SemaphoreType.DMA((4 * (reals - 1),)),
        ],
        compiler_params=pltpu.CompilerParams(
            collective_id=1, has_side_effects=True, vmem_limit_bytes=40 * 1024 * 1024
        ),
    )(held, basis, last)


def place_kernel(snaps, got_ref, core_ref):
    reals = got_ref.shape[0]
    for cell in range(core_ref.shape[0]):
        lanes = slice(cell * snaps, (cell + 1) * snaps)
        core_ref[cell] = jnp.concatenate([got_ref[s, :, lanes] for s in range(reals)], axis=1)


def placed(got, snaps):
    reals, ranks, rows = got.shape
    cells, steps = rows // snaps, 2
    return pl.pallas_call(
        functools.partial(place_kernel, snaps),
        grid=(steps,),
        out_shape=jax.ShapeDtypeStruct((cells, ranks, reals * snaps), jnp.float32),
        in_specs=[pl.BlockSpec((reals, ranks, rows // steps), lambda i: (0, 0, i))],
        out_specs=pl.BlockSpec((cells // steps, ranks, reals * snaps), lambda i: (i, 0, 0)),
        compiler_params=pltpu.CompilerParams(vmem_limit_bytes=32 * 1024 * 1024),
    )(got)


def local(soil_heat_field, seed_subspace):
    reals, depth = lax.axis_size("real"), lax.axis_size("cell") // 2
    held, packed = gathered_gram(soil_heat_field, reals, depth)
    mode_factor, triangle, last = factors(packed, seed_subspace)
    cells, snaps, width = held.shape[1:]
    rows = held.reshape(reals, cells * snaps, width)
    got, corner = projected(rows, mode_factor, last, reals)
    core_tensor = placed(got, snaps).transpose(0, 2, 1)
    first = triangle.shape[0] - corner.shape[0]
    triangle = lax.dynamic_update_slice(triangle, corner, (first, first))
    return (core_tensor, mode_factor, triangle)


def solution(mesh):
    return jax.shard_map(
        local,
        mesh=mesh,
        in_specs=(P("cell", None, "real"), P()),
        out_specs=(P("cell", None, "real"), P(), P()),
        check_vma=False,
    )
```

```python
import functools
import jax
import jax.numpy as jnp
from jax import lax
from jax.experimental import pallas as pl
from jax.experimental.pallas import tpu as pltpu
from jax.sharding import PartitionSpec as P

ITERS = 3
PANEL = 32
GROUP = 8
HI = lax.Precision.HIGHEST


def mm(a, b, dims=((1,), (0,))):
    return lax.dot_general(
        a, b, (dims, ((), ())), precision=HI, preferred_element_type=jnp.float32
    )


def upper_blocks(count):
    return [(i, j) for i in range(count) for j in range(i, count)]


def spread(tile, lane):
    return jnp.broadcast_to(tile[:, lane : lane + 1], tile.shape)


def reciprocal(x):
    guess = pl.reciprocal(x, approx=True)
    return guess * (2.0 - x * guess)


def eliminate(tiles, first_lane):
    sub = lax.broadcasted_iota(jnp.int32, tiles[0][0].shape, 0)
    done = []
    for g in range(len(tiles)):
        lane = first_lane + g * GROUP
        head, rest = tiles[g], tiles[g + 1 :]
        rows = [
            [jnp.broadcast_to(half[i : i + 1, :], half.shape) for half in head]
            for i in range(GROUP)
        ]
        cell = {
            (i, k): spread(rows[i][0], lane + k)
            for i in range(GROUP)
            for k in range(i, GROUP)
        }
        cols = [[spread(t[0], lane + k) for t in rest] for k in range(GROUP)]
        for i in range(GROUP):
            inverse = reciprocal(cell[i, i])
            for k in range(i + 1, GROUP):
                factor = cell[i, k] * inverse
                for q in range(k, GROUP):
                    cell[k, q] = cell[k, q] - factor * cell[i, q]
                rows[k] = [x - factor * y for x, y in zip(rows[k], rows[i])]
                cols[k] = [x - factor * y for x, y in zip(cols[k], cols[i])]
            scaled = [y * inverse for y in rows[i]]
            rest = [
                tuple(x - c * y for x, y in zip(t, scaled)) for t, c in zip(rest, cols[i])
            ]
        tiles = tiles[: g + 1] + rest
        pivots, halves = cell[0, 0], rows[0]
        for i in range(1, GROUP):
            here = sub == i
            pivots = jnp.where(here, cell[i, i], pivots)
            halves = [jnp.where(here, x, y) for x, y in zip(rows[i], halves)]
        scale = lax.rsqrt(pivots)
        halves = [x * scale for x in halves]
        done.append(halves)
    return done


def factor_panels(works, outs, size):
    for p in range(0, size, PANEL):
        for work, out in zip(works, outs):
            tiles = [
                (work[q : q + GROUP, :size], work[q : q + GROUP, size:])
                for q in range(p, p + PANEL, GROUP)
            ]
            for g, (left, right) in enumerate(eliminate(tiles, p)):
                at = p + g * GROUP
                out[at : at + GROUP, :size] = left
                out[at : at + GROUP, size:] = right
            if p + PANEL < size:
                rows = out[p : p + PANEL, :]
                drop = mm(rows[:, :size], rows, ((0,), (0,)))
                work[p + PANEL :, :] = work[p + PANEL :, :] - drop[p + PANEL :, :]


def unpack(packed_ref, gram_ref):
    size = packed_ref.shape[1]
    for number, (i, j) in enumerate(upper_blocks(gram_ref.shape[0] // size)):
        block = packed_ref[number * size : (number + 1) * size, :]
        gram_ref[i * size : (i + 1) * size, j * size : (j + 1) * size] = block
        if i != j:
            gram_ref[j * size : (j + 1) * size, i * size : (i + 1) * size] = block.T


def positions(size):
    row = lax.broadcasted_iota(jnp.int32, (size, size), 0)
    return row, lax.broadcasted_iota(jnp.int32, (size, size), 1)


def triangle_rows(tri_ref, rest, work, out):
    total, size = rest.shape[0], work.shape[0]
    row, col = positions(size)

    def block_rows(block):
        at = pl.multiple_of(block * size, size)
        work[:, :size] = rest[pl.ds(at, size), pl.ds(at, size)]
        work[:, size:] = jnp.where(row == col, 1.0, 0.0).astype(jnp.float32)
        factor_panels([work], [out], size)
        inverse = jnp.where(row >= col, out[:, size:], 0.0)
        strip = mm(inverse, rest[pl.ds(at, size), :])
        rows = at + lax.broadcasted_iota(jnp.int32, (size, total), 0)
        cols = lax.broadcasted_iota(jnp.int32, (size, total), 1)
        strip = jnp.where(cols >= rows, strip, 0.0)
        tri_ref[pl.ds(at, size), :] = strip
        return strip

    def step(block, carry):
        strip = block_rows(block)
        rest[...] = rest[...] - mm(strip, strip, ((0,), (0,)))
        return carry

    blocks = total // size
    lax.fori_loop(0, blocks - 1, step, 0)
    block_rows(blocks - 1)


def basis_kernel(packed_ref, seed_ref, basis_ref, gram_ref, image, work, out):
    size = seed_ref.shape[1]
    row, col = positions(size)
    unpack(packed_ref, gram_ref)
    basis_ref[...] = seed_ref[...]

    def step(index, carry):
        image[...] = mm(gram_ref[...], basis_ref[...])
        work[:, :size] = mm(image[...], image[...], ((0,), (0,)))
        work[:, size:] = jnp.where(row == col, 1.0, 0.0).astype(jnp.float32)
        factor_panels([work], [out], size)
        inverse = jnp.where(row >= col, out[:, size:], 0.0)
        basis_ref[...] = mm(image[...], inverse, ((1,), (1,)))
        return carry

    lax.fori_loop(0, ITERS, step, 0)


def iterated(packed, seed_subspace):
    total, size = seed_subspace.shape
    vmem = pl.BlockSpec(memory_space=pltpu.VMEM)
    return pl.pallas_call(
        basis_kernel,
        out_shape=jax.ShapeDtypeStruct((total, size), jnp.float32),
        in_specs=[vmem] * 2,
        out_specs=vmem,
        scratch_shapes=[
            pltpu.VMEM((total, total), jnp.float32),
            pltpu.VMEM((total, size), jnp.float32),
            pltpu.VMEM((size, 2 * size), jnp.float32),
            pltpu.VMEM((size, 2 * size), jnp.float32),
        ],
        compiler_params=pltpu.CompilerParams(vmem_limit_bytes=32 * 1024 * 1024),
    )(packed, seed_subspace)


MESH = pl.DeviceIdType.MESH


def greet(peers):
    barrier = pltpu.get_barrier_semaphore()
    for peer in peers:
        pl.semaphore_signal(barrier, inc=1, device_id=peer, device_id_type=MESH)
    pl.semaphore_wait(barrier, len(peers))


def send(src, dst, sems, slot, peer):
    copy = pltpu.make_async_remote_copy(
        src_ref=src,
        dst_ref=dst,
        send_sem=sems[0].at[slot],
        recv_sem=sems[1].at[slot],
        device_id=peer,
        device_id_type=MESH,
    )
    copy.start()
    return copy


def gram_kernel(
    reals, depth, chunks, field_ref, stored_ref, out_ref, held_ref, acc, packed,
    from_core, half, from_real, quarter, from_depth, own_sem, store_sem,
    field_send, field_recv, sum_send, sum_recv, gather_send, gather_recv,
):
    r, cell = lax.axis_index("real"), lax.axis_index("cell")
    z, c = cell // 2, cell % 2
    cells, snaps, width = held_ref.shape[1:]
    real_peers = [lax.rem(r + d, reals) for d in range(1, reals)]
    depth_peers = [lax.rem(z + d, depth) for d in range(1, depth)]
    to_core = {"real": r, "cell": z * 2 + 1 - c}
    to_real = [{"real": q, "cell": cell} for q in real_peers]
    to_depth = [{"real": r, "cell": q * 2 + c} for q in depth_peers]
    greet([to_core] + to_real + to_depth)

    step = cells // chunks
    moves = []
    for k in range(chunks):
        own = pltpu.make_async_copy(
            field_ref.at[pl.ds(k * step, step), pl.ds(r * snaps, snaps), :],
            held_ref.at[r, pl.ds(k * step, step)],
            own_sem.at[k],
        )
        own.start()
        moves.append([own])
        for d, (q, peer) in enumerate(zip(real_peers, to_real)):
            moves[k].append(
                send(
                    field_ref.at[pl.ds(k * step, step), pl.ds(q * snaps, snaps), :],
                    held_ref.at[r, pl.ds(k * step, step)],
                    (field_send, field_recv),
                    k * (reals - 1) + d,
                    peer,
                )
            )
    total_rows = cells * snaps * reals * depth * 2
    stores = []
    for k in range(chunks):
        moves[k][0].wait()
        for copy in moves[k][1:]:
            copy.wait_recv()
        store = pltpu.make_async_copy(
            held_ref.at[:, pl.ds(k * step, step)],
            stored_ref.at[:, pl.ds(k * step, step)],
            store_sem.at[k],
        )
        store.start()
        stores.append(store)
        rows = jnp.concatenate(
            [
                held_ref[s, k * step : (k + 1) * step].reshape(step * snaps, width)
                for s in range(reals)
            ],
            axis=1,
        )
        part = mm(rows, rows, ((0,), (0,)))
        acc[...] = part if k == 0 else acc[...] + part
    for k in range(chunks):
        for copy in moves[k][1:]:
            copy.wait_send()

    blocks = upper_blocks(reals)
    for number, (i, j) in enumerate(blocks):
        packed[number * width : (number + 1) * width, :] = (
            acc[i * width : (i + 1) * width, j * width : (j + 1) * width] / total_rows
        )
    used = len(blocks) * width
    if packed.shape[0] > used:
        packed[used:, :] = jnp.zeros((packed.shape[0] - used, width), jnp.float32)

    sums = (sum_send, sum_recv)
    h, q, e = half.shape[0], quarter.shape[0], from_depth.shape[1]
    copy = send(packed.at[pl.ds((1 - c) * h, h)], from_core, sums, 0, to_core)
    copy.wait()
    half[...] = packed[pl.ds(pl.multiple_of(c * h, 8), h), :] + from_core[...]
    copies = [
        send(half.at[pl.ds(p * q, q)], from_real.at[d], sums, 1 + d, peer)
        for d, (p, peer) in enumerate(zip(real_peers, to_real))
    ]
    for copy in copies:
        copy.wait()
    value = half[pl.ds(pl.multiple_of(r * q, 8), q), :]
    for d in range(reals - 1):
        value = value + from_real[d]
    quarter[...] = value
    copies = [
        send(quarter.at[pl.ds(p * e, e)], from_depth.at[d], sums, reals + d, peer)
        for d, (p, peer) in enumerate(zip(depth_peers, to_depth))
    ]
    for copy in copies:
        copy.wait()
    value = quarter[pl.ds(pl.multiple_of(z * e, 8), e), :]
    for d in range(depth - 1):
        value = value + from_depth[d]

    gathers = (gather_send, gather_recv)
    base = c * h + r * q
    mine = pl.multiple_of(base + z * e, 8)
    out_ref[pl.ds(mine, e), :] = value
    for first, count, slot, peers in (
        (mine, e, reals, to_depth),
        (base, q, 1, to_real),
        (c * h, h, 0, [to_core]),
    ):
        part = out_ref.at[pl.ds(first, count)]
        copies = [send(part, part, gathers, slot + d, peer) for d, peer in enumerate(peers)]
        for copy in copies:
            copy.wait()
    for store in stores:
        store.wait()


def gathered_gram(field, reals, depth):
    cells, snaps, width = field.shape
    snaps //= reals
    chunks = 8
    used = len(upper_blocks(reals)) * width
    e = -(-used // (2 * reals * depth * 8)) * 8
    q = e * depth
    h = q * reals
    peers = reals + depth - 1
    f32 = jnp.float32
    dma = pltpu.SemaphoreType.DMA
    vmem = pl.BlockSpec(memory_space=pltpu.VMEM)
    return pl.pallas_call(
        functools.partial(gram_kernel, reals, depth, chunks),
        out_shape=(
            jax.ShapeDtypeStruct((reals, cells, snaps, width), f32),
            jax.ShapeDtypeStruct((2 * h, width), f32),
        ),
        in_specs=[pl.BlockSpec(memory_space=pl.ANY)],
        out_specs=[pl.BlockSpec(memory_space=pl.ANY), vmem],
        scratch_shapes=[
            pltpu.VMEM((reals, cells, snaps, width), f32),
            pltpu.VMEM((reals * width, reals * width), f32),
            pltpu.VMEM((2 * h, width), f32),
            pltpu.VMEM((h, width), f32),
            pltpu.VMEM((h, width), f32),
            pltpu.VMEM((reals - 1, q, width), f32),
            pltpu.VMEM((q, width), f32),
            pltpu.VMEM((depth - 1, e, width), f32),
            dma((chunks,)),
            dma((chunks,)),
            dma((chunks * (reals - 1),)),
            dma((chunks * (reals - 1),)),
            dma((peers,)),
            dma((peers,)),
            dma((peers,)),
            dma((peers,)),
        ],
        compiler_params=pltpu.CompilerParams(
            collective_id=0, has_side_effects=True, vmem_limit_bytes=60 * 1024 * 1024
        ),
    )(field)


def core_kernel(
    reals, parts, stored_ref, basis_ref, packed_ref, got_ref, tri_ref,
    held_ref, sending, rest, work, out, load_sem, send_sem, recv_sem,
):
    r, cell = lax.axis_index("real"), lax.axis_index("cell")
    rows, width = stored_ref.shape[1:]
    count = rows // parts
    loads = []
    for part in range(parts):
        place = pl.ds(part * count, count)
        load = pltpu.make_async_copy(
            stored_ref.at[:, place], held_ref.at[:, place], load_sem.at[part]
        )
        load.start()
        loads.append(load)
    peers = [lax.rem(r + d, reals) for d in range(1, reals)]
    places = [{"real": q, "cell": cell} for q in peers]
    greet(places)
    ranks = got_ref.shape[1]
    copies = []
    for part in range(parts):
        first = part * count
        loads[part].wait()
        value = mm(held_ref[0, first : first + count, :], basis_ref[:width, :])
        for s in range(1, reals):
            value = value + mm(
                held_ref[s, first : first + count, :], basis_ref[s * width : (s + 1) * width, :]
            )
        turned = value.T
        for s in range(reals):
            sending[s, :, first : first + count] = turned[s * ranks : (s + 1) * ranks, :]
        lanes = pl.ds(first, count)
        for d, (q, place) in enumerate(zip(peers, places)):
            copies.append(
                send(
                    sending.at[q, :, lanes],
                    got_ref.at[r, :, lanes],
                    (send_sem, recv_sem),
                    part * (reals - 1) + d,
                    place,
                )
            )
    got_ref[pl.ds(r, 1)] = sending[pl.ds(r, 1)]
    unpack(packed_ref, rest)
    triangle_rows(tri_ref, rest, work, out)
    for copy in copies:
        copy.wait()


def projected(stored, basis, packed, reals):
    rows, width = stored.shape[1:]
    total, rank = basis.shape
    shape = (reals, rank // reals, rows)
    parts = 4
    dma = pltpu.SemaphoreType.DMA
    vmem = pl.BlockSpec(memory_space=pltpu.VMEM)
    return pl.pallas_call(
        functools.partial(core_kernel, reals, parts),
        out_shape=(
            jax.ShapeDtypeStruct(shape, jnp.float32),
            jax.ShapeDtypeStruct((total, total), jnp.float32),
        ),
        in_specs=[pl.BlockSpec(memory_space=pl.ANY), vmem, vmem],
        out_specs=[vmem] * 2,
        scratch_shapes=[
            pltpu.VMEM(stored.shape, jnp.float32),
            pltpu.VMEM(shape, jnp.float32),
            pltpu.VMEM((total, total), jnp.float32),
            pltpu.VMEM((width, 2 * width), jnp.float32),
            pltpu.VMEM((width, 2 * width), jnp.float32),
            dma((parts,)),
            dma((parts * (reals - 1),)),
            dma((parts * (reals - 1),)),
        ],
        compiler_params=pltpu.CompilerParams(
            collective_id=1, has_side_effects=True, vmem_limit_bytes=60 * 1024 * 1024
        ),
    )(stored, basis, packed)


def place_kernel(snaps, got_ref, core_ref):
    reals = got_ref.shape[0]
    for cell in range(core_ref.shape[0]):
        lanes = slice(cell * snaps, (cell + 1) * snaps)
        core_ref[cell] = jnp.concatenate([got_ref[s, :, lanes] for s in range(reals)], axis=1)


def placed(got, snaps):
    reals, ranks, rows = got.shape
    cells, steps = rows // snaps, 2
    return pl.pallas_call(
        functools.partial(place_kernel, snaps),
        grid=(steps,),
        out_shape=jax.ShapeDtypeStruct((cells, ranks, reals * snaps), jnp.float32),
        in_specs=[pl.BlockSpec((reals, ranks, rows // steps), lambda i: (0, 0, i))],
        out_specs=pl.BlockSpec((cells // steps, ranks, reals * snaps), lambda i: (i, 0, 0)),
        compiler_params=pltpu.CompilerParams(vmem_limit_bytes=32 * 1024 * 1024),
    )(got)


def local(soil_heat_field, seed_subspace):
    reals, depth = lax.axis_size("real"), lax.axis_size("cell") // 2
    stored, packed = gathered_gram(soil_heat_field, reals, depth)
    mode_factor = iterated(packed, seed_subspace)
    cells, snaps, width = stored.shape[1:]
    rows = stored.reshape(reals, cells * snaps, width)
    got, triangle = projected(rows, mode_factor, packed, reals)
    core_tensor = placed(got, snaps).transpose(0, 2, 1)
    return (core_tensor, mode_factor, triangle)


def solution(mesh):
    return jax.shard_map(
        local,
        mesh=mesh,
        in_specs=(P("cell", None, "real"), P()),
        out_specs=(P("cell", None, "real"), P(), P()),
        check_vma=False,
    )
```

```python
import functools
import jax
import jax.numpy as jnp
from jax import lax
from jax.experimental import pallas as pl
from jax.experimental.pallas import tpu as pltpu
from jax.sharding import PartitionSpec as P

ITERS = 3
PANEL = 32
GROUP = 8
HI = lax.Precision.HIGHEST


def mm(a, b, dims=((1,), (0,))):
    return lax.dot_general(
        a, b, (dims, ((), ())), precision=HI, preferred_element_type=jnp.float32
    )


def upper_blocks(count):
    return [(i, j) for i in range(count) for j in range(i, count)]


def spread(tile, lane):
    return jnp.broadcast_to(tile[:, lane : lane + 1], tile.shape)


def reciprocal(x):
    guess = pl.reciprocal(x, approx=True)
    return guess * (2.0 - x * guess)


def eliminate(tiles, first_lane):
    sub = lax.broadcasted_iota(jnp.int32, tiles[0][0].shape, 0)
    done = []
    for g in range(len(tiles)):
        lane = first_lane + g * GROUP
        head, rest = tiles[g], tiles[g + 1 :]
        rows = [
            [jnp.broadcast_to(half[i : i + 1, :], half.shape) for half in head]
            for i in range(GROUP)
        ]
        cell = {
            (i, k): spread(rows[i][0], lane + k)
            for i in range(GROUP)
            for k in range(i, GROUP)
        }
        cols = [[spread(t[0], lane + k) for t in rest] for k in range(GROUP)]
        for i in range(GROUP):
            inverse = reciprocal(cell[i, i])
            for k in range(i + 1, GROUP):
                factor = cell[i, k] * inverse
                for q in range(k, GROUP):
                    cell[k, q] = cell[k, q] - factor * cell[i, q]
                rows[k] = [x - factor * y for x, y in zip(rows[k], rows[i])]
                cols[k] = [x - factor * y for x, y in zip(cols[k], cols[i])]
            scaled = [y * inverse for y in rows[i]]
            rest = [
                tuple(x - c * y for x, y in zip(t, scaled)) for t, c in zip(rest, cols[i])
            ]
        tiles = tiles[: g + 1] + rest
        pivots, halves = cell[0, 0], rows[0]
        for i in range(1, GROUP):
            here = sub == i
            pivots = jnp.where(here, cell[i, i], pivots)
            halves = [jnp.where(here, x, y) for x, y in zip(rows[i], halves)]
        scale = lax.rsqrt(pivots)
        halves = [x * scale for x in halves]
        done.append(halves)
    return done


def factor_panels(works, outs, size):
    for p in range(0, size, PANEL):
        for work, out in zip(works, outs):
            tiles = [
                (work[q : q + GROUP, :size], work[q : q + GROUP, size:])
                for q in range(p, p + PANEL, GROUP)
            ]
            for g, (left, right) in enumerate(eliminate(tiles, p)):
                at = p + g * GROUP
                out[at : at + GROUP, :size] = left
                out[at : at + GROUP, size:] = right
            if p + PANEL < size:
                rows = out[p : p + PANEL, :]
                drop = mm(rows[:, :size], rows, ((0,), (0,)))
                work[p + PANEL :, :] = work[p + PANEL :, :] - drop[p + PANEL :, :]


def factors_kernel(packed_ref, seed_ref, basis_ref, tri_ref, last_ref, gram_ref, rest, image, work_a, out_a, work_b, out_b):
    size = seed_ref.shape[1]
    total = seed_ref.shape[0]
    for number, (i, j) in enumerate(upper_blocks(total // size)):
        block = packed_ref[number * size : (number + 1) * size, :]
        gram_ref[i * size : (i + 1) * size, j * size : (j + 1) * size] = block
        if i != j:
            gram_ref[j * size : (j + 1) * size, i * size : (i + 1) * size] = block.T
    row = lax.broadcasted_iota(jnp.int32, (size, size), 0)
    col = lax.broadcasted_iota(jnp.int32, (size, size), 1)
    eye = jnp.where(row == col, 1.0, 0.0).astype(jnp.float32)
    rest[...] = gram_ref[...]
    basis_ref[...] = seed_ref[...]

    def triangle_start(block):
        at = pl.multiple_of(block * size, size)
        work_b[:, :size] = rest[pl.ds(at, size), pl.ds(at, size)]
        work_b[:, size:] = eye

    def triangle_end(block):
        at = pl.multiple_of(block * size, size)
        inverse = jnp.where(row >= col, out_b[:, size:], 0.0)
        strip = mm(inverse, rest[pl.ds(at, size), :])
        rows = at + lax.broadcasted_iota(jnp.int32, (size, total), 0)
        cols = lax.broadcasted_iota(jnp.int32, (size, total), 1)
        strip = jnp.where(cols >= rows, strip, 0.0)
        tri_ref[pl.ds(at, size), :] = strip
        return strip

    def step(index, carry):
        image[...] = mm(gram_ref[...], basis_ref[...])
        work_a[:, :size] = mm(image[...], image[...], ((0,), (0,)))
        work_a[:, size:] = eye
        triangle_start(index)
        factor_panels([work_a, work_b], [out_a, out_b], size)
        inverse = jnp.where(row >= col, out_a[:, size:], 0.0)
        basis_ref[...] = mm(image[...], inverse, ((1,), (1,)))
        strip = triangle_end(index)
        rest[...] = rest[...] - mm(strip, strip, ((0,), (0,)))
        return carry

    blocks = total // size
    lax.fori_loop(0, ITERS, step, 0)
    for block in range(ITERS, blocks - 1):
        triangle_start(block)
        factor_panels([work_b], [out_b], size)
        strip = triangle_end(block)
        rest[...] = rest[...] - mm(strip, strip, ((0,), (0,)))
    tri_ref[total - size :, :] = jnp.zeros((size, total), jnp.float32)
    last_ref[...] = rest[total - size :, total - size :]


def factors(packed, seed_subspace):
    total, size = seed_subspace.shape
    vmem = pl.BlockSpec(memory_space=pltpu.VMEM)
    return pl.pallas_call(
        factors_kernel,
        out_shape=(
            jax.ShapeDtypeStruct((total, size), jnp.float32),
            jax.ShapeDtypeStruct((total, total), jnp.float32),
            jax.ShapeDtypeStruct((size, size), jnp.float32),
        ),
        in_specs=[vmem] * 2,
        out_specs=[vmem] * 3,
        scratch_shapes=[
            pltpu.VMEM((total, total), jnp.float32),
            pltpu.VMEM((total, total), jnp.float32),
            pltpu.VMEM((total, size), jnp.float32),
        ]
        + [pltpu.VMEM((size, 2 * size), jnp.float32)] * 4,
        compiler_params=pltpu.CompilerParams(vmem_limit_bytes=32 * 1024 * 1024),
    )(packed, seed_subspace)


MESH = pl.DeviceIdType.MESH


def greet(peers):
    barrier = pltpu.get_barrier_semaphore()
    for peer in peers:
        pl.semaphore_signal(barrier, inc=1, device_id=peer, device_id_type=MESH)
    pl.semaphore_wait(barrier, len(peers))


def send(src, dst, sems, slot, peer):
    copy = pltpu.make_async_remote_copy(
        src_ref=src,
        dst_ref=dst,
        send_sem=sems[0].at[slot],
        recv_sem=sems[1].at[slot],
        device_id=peer,
        device_id_type=MESH,
    )
    copy.start()
    return copy


def gram_kernel(
    reals, depth, chunks, field_ref, stored_ref, out_ref, held_ref, acc, packed,
    from_core, half, from_real, quarter, from_depth, own_sem, store_sem,
    field_send, field_recv, sum_send, sum_recv, gather_send, gather_recv,
):
    r, cell = lax.axis_index("real"), lax.axis_index("cell")
    z, c = cell // 2, cell % 2
    cells, snaps, width = held_ref.shape[1:]
    real_peers = [lax.rem(r + d, reals) for d in range(1, reals)]
    depth_peers = [lax.rem(z + d, depth) for d in range(1, depth)]
    to_core = {"real": r, "cell": z * 2 + 1 - c}
    to_real = [{"real": q, "cell": cell} for q in real_peers]
    to_depth = [{"real": r, "cell": q * 2 + c} for q in depth_peers]
    greet([to_core] + to_real + to_depth)

    step = cells // chunks
    moves = []
    for k in range(chunks):
        own = pltpu.make_async_copy(
            field_ref.at[pl.ds(k * step, step), pl.ds(r * snaps, snaps), :],
            held_ref.at[r, pl.ds(k * step, step)],
            own_sem.at[k],
        )
        own.start()
        moves.append([own])
        for d, (q, peer) in enumerate(zip(real_peers, to_real)):
            moves[k].append(
                send(
                    field_ref.at[pl.ds(k * step, step), pl.ds(q * snaps, snaps), :],
                    held_ref.at[r, pl.ds(k * step, step)],
                    (field_send, field_recv),
                    k * (reals - 1) + d,
                    peer,
                )
            )
    total_rows = cells * snaps * reals * depth * 2
    stores = []
    for k in range(chunks):
        moves[k][0].wait()
        for copy in moves[k][1:]:
            copy.wait_recv()
        store = pltpu.make_async_copy(
            held_ref.at[:, pl.ds(k * step, step)],
            stored_ref.at[:, pl.ds(k * step, step)],
            store_sem.at[k],
        )
        store.start()
        stores.append(store)
        rows = jnp.concatenate(
            [
                held_ref[s, k * step : (k + 1) * step].reshape(step * snaps, width)
                for s in range(reals)
            ],
            axis=1,
        )
        part = mm(rows, rows, ((0,), (0,)))
        acc[...] = part if k == 0 else acc[...] + part
    for k in range(chunks):
        for copy in moves[k][1:]:
            copy.wait_send()

    blocks = upper_blocks(reals)
    for number, (i, j) in enumerate(blocks):
        packed[number * width : (number + 1) * width, :] = (
            acc[i * width : (i + 1) * width, j * width : (j + 1) * width] / total_rows
        )
    used = len(blocks) * width
    if packed.shape[0] > used:
        packed[used:, :] = jnp.zeros((packed.shape[0] - used, width), jnp.float32)

    sums = (sum_send, sum_recv)
    h, q, e = half.shape[0], quarter.shape[0], from_depth.shape[1]
    copy = send(packed.at[pl.ds((1 - c) * h, h)], from_core, sums, 0, to_core)
    copy.wait()
    half[...] = packed[pl.ds(pl.multiple_of(c * h, 8), h), :] + from_core[...]
    copies = [
        send(half.at[pl.ds(p * q, q)], from_real.at[d], sums, 1 + d, peer)
        for d, (p, peer) in enumerate(zip(real_peers, to_real))
    ]
    for copy in copies:
        copy.wait()
    value = half[pl.ds(pl.multiple_of(r * q, 8), q), :]
    for d in range(reals - 1):
        value = value + from_real[d]
    quarter[...] = value
    copies = [
        send(quarter.at[pl.ds(p * e, e)], from_depth.at[d], sums, reals + d, peer)
        for d, (p, peer) in enumerate(zip(depth_peers, to_depth))
    ]
    for copy in copies:
        copy.wait()
    value = quarter[pl.ds(pl.multiple_of(z * e, 8), e), :]
    for d in range(depth - 1):
        value = value + from_depth[d]

    gathers = (gather_send, gather_recv)
    base = c * h + r * q
    mine = pl.multiple_of(base + z * e, 8)
    out_ref[pl.ds(mine, e), :] = value
    for first, count, slot, peers in (
        (mine, e, reals, to_depth),
        (base, q, 1, to_real),
        (c * h, h, 0, [to_core]),
    ):
        part = out_ref.at[pl.ds(first, count)]
        copies = [send(part, part, gathers, slot + d, peer) for d, peer in enumerate(peers)]
        for copy in copies:
            copy.wait()
    for store in stores:
        store.wait()


def gathered_gram(field, reals, depth):
    cells, snaps, width = field.shape
    snaps //= reals
    chunks = 8
    used = len(upper_blocks(reals)) * width
    e = -(-used // (2 * reals * depth * 8)) * 8
    q = e * depth
    h = q * reals
    peers = reals + depth - 1
    f32 = jnp.float32
    dma = pltpu.SemaphoreType.DMA
    vmem = pl.BlockSpec(memory_space=pltpu.VMEM)
    return pl.pallas_call(
        functools.partial(gram_kernel, reals, depth, chunks),
        out_shape=(
            jax.ShapeDtypeStruct((reals, cells, snaps, width), f32),
            jax.ShapeDtypeStruct((2 * h, width), f32),
        ),
        in_specs=[pl.BlockSpec(memory_space=pl.ANY)],
        out_specs=[pl.BlockSpec(memory_space=pl.ANY), vmem],
        scratch_shapes=[
            pltpu.VMEM((reals, cells, snaps, width), f32),
            pltpu.VMEM((reals * width, reals * width), f32),
            pltpu.VMEM((2 * h, width), f32),
            pltpu.VMEM((h, width), f32),
            pltpu.VMEM((h, width), f32),
            pltpu.VMEM((reals - 1, q, width), f32),
            pltpu.VMEM((q, width), f32),
            pltpu.VMEM((depth - 1, e, width), f32),
            dma((chunks,)),
            dma((chunks,)),
            dma((chunks * (reals - 1),)),
            dma((chunks * (reals - 1),)),
            dma((peers,)),
            dma((peers,)),
            dma((peers,)),
            dma((peers,)),
        ],
        compiler_params=pltpu.CompilerParams(
            collective_id=0, has_side_effects=True, vmem_limit_bytes=60 * 1024 * 1024
        ),
    )(field)


def core_kernel(
    reals, parts, stored_ref, basis_ref, last_ref, got_ref, corner_ref,
    held_ref, sending, work, out, load_sem, send_sem, recv_sem,
):
    r, cell = lax.axis_index("real"), lax.axis_index("cell")
    rows, width = stored_ref.shape[1:]
    count = rows // parts
    loads = []
    for part in range(parts):
        place = pl.ds(part * count, count)
        load = pltpu.make_async_copy(
            stored_ref.at[:, place], held_ref.at[:, place], load_sem.at[part]
        )
        load.start()
        loads.append(load)
    peers = [lax.rem(r + d, reals) for d in range(1, reals)]
    places = [{"real": q, "cell": cell} for q in peers]
    greet(places)
    ranks = got_ref.shape[1]
    copies = []
    for part in range(parts):
        first = part * count
        loads[part].wait()
        value = mm(held_ref[0, first : first + count, :], basis_ref[:width, :])
        for s in range(1, reals):
            value = value + mm(
                held_ref[s, first : first + count, :], basis_ref[s * width : (s + 1) * width, :]
            )
        turned = value.T
        for s in range(reals):
            sending[s, :, first : first + count] = turned[s * ranks : (s + 1) * ranks, :]
        lanes = pl.ds(first, count)
        for d, (q, place) in enumerate(zip(peers, places)):
            copies.append(
                send(
                    sending.at[q, :, lanes],
                    got_ref.at[r, :, lanes],
                    (send_sem, recv_sem),
                    part * (reals - 1) + d,
                    place,
                )
            )
    got_ref[pl.ds(r, 1)] = sending[pl.ds(r, 1)]
    size = last_ref.shape[0]
    row = lax.broadcasted_iota(jnp.int32, (size, size), 0)
    col = lax.broadcasted_iota(jnp.int32, (size, size), 1)
    work[:, :size] = last_ref[...]
    work[:, size:] = jnp.where(row == col, 1.0, 0.0).astype(jnp.float32)
    factor_panels([work], [out], size)
    corner_ref[...] = jnp.where(col >= row, out[:, :size], 0.0)
    for copy in copies:
        copy.wait()


def projected(held, basis, last, reals):
    rows, width = held.shape[1:]
    rank = basis.shape[1]
    size = last.shape[0]
    shape = (reals, rank // reals, rows)
    parts = 4
    dma = pltpu.SemaphoreType.DMA
    vmem = pl.BlockSpec(memory_space=pltpu.VMEM)
    return pl.pallas_call(
        functools.partial(core_kernel, reals, parts),
        out_shape=(
            jax.ShapeDtypeStruct(shape, jnp.float32),
            jax.ShapeDtypeStruct(last.shape, jnp.float32),
        ),
        in_specs=[pl.BlockSpec(memory_space=pl.ANY), vmem, vmem],
        out_specs=[vmem] * 2,
        scratch_shapes=[
            pltpu.VMEM(held.shape, jnp.float32),
            pltpu.VMEM(shape, jnp.float32),
            pltpu.VMEM((size, 2 * size), jnp.float32),
            pltpu.VMEM((size, 2 * size), jnp.float32),
            dma((parts,)),
            dma((parts * (reals - 1),)),
            dma((parts * (reals - 1),)),
        ],
        compiler_params=pltpu.CompilerParams(
            collective_id=1, has_side_effects=True, vmem_limit_bytes=60 * 1024 * 1024
        ),
    )(held, basis, last)


def place_kernel(snaps, got_ref, core_ref):
    reals = got_ref.shape[0]
    for cell in range(core_ref.shape[0]):
        lanes = slice(cell * snaps, (cell + 1) * snaps)
        core_ref[cell] = jnp.concatenate([got_ref[s, :, lanes] for s in range(reals)], axis=1)


def placed(got, snaps):
    reals, ranks, rows = got.shape
    cells, steps = rows // snaps, 2
    return pl.pallas_call(
        functools.partial(place_kernel, snaps),
        grid=(steps,),
        out_shape=jax.ShapeDtypeStruct((cells, ranks, reals * snaps), jnp.float32),
        in_specs=[pl.BlockSpec((reals, ranks, rows // steps), lambda i: (0, 0, i))],
        out_specs=pl.BlockSpec((cells // steps, ranks, reals * snaps), lambda i: (i, 0, 0)),
        compiler_params=pltpu.CompilerParams(vmem_limit_bytes=32 * 1024 * 1024),
    )(got)


def local(soil_heat_field, seed_subspace):
    reals, depth = lax.axis_size("real"), lax.axis_size("cell") // 2
    held, packed = gathered_gram(soil_heat_field, reals, depth)
    mode_factor, triangle, last = factors(packed, seed_subspace)
    cells, snaps, width = held.shape[1:]
    rows = held.reshape(reals, cells * snaps, width)
    got, corner = projected(rows, mode_factor, last, reals)
    core_tensor = placed(got, snaps).transpose(0, 2, 1)
    first = triangle.shape[0] - corner.shape[0]
    triangle = lax.dynamic_update_slice(triangle, corner, (first, first))
    return (core_tensor, mode_factor, triangle)


def solution(mesh):
    return jax.shard_map(
        local,
        mesh=mesh,
        in_specs=(P("cell", None, "real"), P()),
        out_specs=(P("cell", None, "real"), P(), P()),
        check_vma=False,
    )
```
